256 devices in a mesh: row: 32 (over z_lo, x, core), col: 8 (over y, z_hi).
Axes of the slice: x: 4, y: 4, z: 8 (z_hi: 2, z_lo: 4; z = z_hi * 4 + z_lo), core: 2. Of those that a mesh axis runs over, the one named last changes fastest.
Arguments:
- tokens: bfloat16 [512, 12288], P('row', 'col'), may hold values from -6 to 6
- weight_in: bfloat16 [12288, 49152], P('col', 'row'), may hold values from -0.0546875 to 0.0546875
- weight_out: bfloat16 [49152, 12288], P('row', 'col'), may hold values from -0.02734375 to 0.02734375
- grad_out: bfloat16 [512, 12288], P('row', 'col'), may hold values from -6 to 6
Outputs:
- output: bfloat16 [512, 12288], P('row', 'col')
- grad_tokens: bfloat16 [512, 12288], P('row', 'col')
The draws below stay inside these ranges and needn't reach their ends.
All inputs are finite; a program needn't handle non-finite values.
Results may differ from the reference program's by a relative error of at most 0.0049.
Values may be sent and summed in bfloat16 or wider, within the bound.
A program may use at most 64 MiB of HBM per device.

```python
import jax
import jax.numpy as jnp
from jax import lax

D = 12288
FF = 49152
TOKENS = 512


def levels(stream_key, dims, pieces, low, largest):
    def one(dim, shards_of):
        heights = jax.random.uniform(jax.random.fold_in(jax.random.fold_in(stream_key, 6), dim), (shards_of,), jnp.float32, low / len(pieces), largest / len(pieces))
        return jnp.repeat(jnp.exp(heights), dims[dim] // shards_of).reshape((-1,) + (1,) * (len(dims) - dim - 1))

    level = one(*pieces[0])
    for cut in pieces[1:]:
        level = level * one(*cut)
    return level


def scatter_about(own_key, dims, deviation, bound, split=(), held_as=jnp.bfloat16):
    gain = levels(own_key, dims, split, -0.22, 0.18) if split else 1.0
    drawn = jax.random.normal(own_key, dims, jnp.float32) * deviation * gain
    return jnp.minimum(jnp.maximum(drawn, -bound), bound).astype(held_as)


def setup_inputs(seed: int = 0) -> dict:
    seeds = jax.random.split(jax.random.key(seed), 5)
    return {
        "tokens": scatter_about(seeds[0], (TOKENS, D), 1.0, 6.0, ((0, 32), (1, 8))),
        "weight_in": scatter_about(seeds[1], (D, FF), D ** -0.5, 0.0546875, ((0, 8), (1, 32))),
        "weight_out": scatter_about(seeds[2], (FF, D), FF ** -0.5, 0.02734375, ((0, 32), (1, 8))),
        "grad_out": scatter_about(seeds[3], (TOKENS, D), 1.0, 6.0, ((0, 32), (1, 8))),
    }


tanh_scale = 0.7978845608028654
cube_weight = 0.044715


def gelu_tanh(hidden):
    inner = tanh_scale * (hidden + cube_weight * hidden * hidden * hidden)
    return 0.5 * hidden * (1.0 + jnp.tanh(inner))


def gelu_slope(hidden):
    inner = tanh_scale * (hidden + cube_weight * hidden * hidden * hidden)
    tangent = jnp.tanh(inner)
    return 0.5 * (1.0 + tangent) + 0.5 * hidden * (1.0 - tangent * tangent) * tanh_scale * (1.0 + 3.0 * cube_weight * hidden * hidden)


def reference(tokens, weight_in, weight_out, grad_out):
    hidden = jnp.dot(tokens, weight_in, preferred_element_type=jnp.float32)
    activation = gelu_tanh(hidden).astype(jnp.bfloat16)
    output = jnp.dot(activation, weight_out, preferred_element_type=jnp.float32).astype(jnp.bfloat16)
    act_grad = lax.dot_general(grad_out, weight_out, (((1,), (1,)), ((), ())), preferred_element_type=jnp.float32)
    hid_grad = (act_grad * gelu_slope(hidden)).astype(jnp.bfloat16)
    grad_tokens = lax.dot_general(hid_grad, weight_in, (((1,), (1,)), ((), ())), preferred_element_type=jnp.float32).astype(jnp.bfloat16)
    return output, grad_tokens
```

```python
import functools

import jax
import jax.numpy as jnp
from jax import lax
from jax.experimental import pallas as pl
from jax.experimental.pallas import tpu as pltpu
from jax.sharding import PartitionSpec as P

MESH = pl.DeviceIdType.MESH
f32, bf16 = jnp.float32, jnp.bfloat16
tanh_scale = 0.7978845608028654
cube_weight = 0.044715

W = 1536
R = 16
NZ = 1
PAIRS = 4 // NZ
N = 2 * PAIRS
M = 128 * NZ
XB, YB, HB = M // 8, M // 4, M // 8
TILE = 256


def columns(step):
    return pl.ds(pl.multiple_of(step * TILE, TILE), TILE)


def rows(start, size):
    return pl.ds(pl.multiple_of(start, R), size)


def kernel(
    tok, grad, wi_hbm, wo_hbm, out, gout,
    wi, wo, wit, wot, xg, part, ysend, yrm, yrp, ycomb, ysum, zsend, zrecv, hid, ag,
    crecv, xsend, xrecv, zrsum, zosend, zorecv,
    w_sem, own_sem, az_s, az_r, ax_s, ax_r, ac_s, ac_r, c_s, cm_r, cp_r, d_s, d_r, f_s, f_r,
    g_s, gm_r, gp_r, ic_s, ic_r, ix_s, ix_r, iz_s, iz_r,
):
    row, col = lax.axis_index("row"), lax.axis_index("col")
    core, x, zl = row % 2, (row // 2) % 4, row // 8
    y, zh = col // 2, col % 2

    def device(x=x, zl=zl, core=core, y=y, zh=zh):
        return ((zl * 4 + x) * 2 + core, y * 2 + zh)

    def ring(i, k):
        return (i + k) % 4

    xs = [device(x=ring(x, k)) for k in (1, 2, 3)]
    zs = [device(zl=ring(zl, k)) for k in (1, 2, 3)]
    sibling = device(core=1 - core)
    up, down = device(y=ring(y, 1)), device(y=ring(y, 3))
    far = device(zh=1 - zh)

    started = []

    def send(src, dst, s_sem, r_sem, to):
        copy = pltpu.make_async_remote_copy(
            src_ref=src, dst_ref=dst, send_sem=s_sem, recv_sem=r_sem,
            device_id=to, device_id_type=MESH,
        )
        copy.start()
        started.append(copy)

    def arrived(ref, sem):
        pltpu.make_async_copy(ref, ref, sem).wait()

    loads = [
        pltpu.make_async_copy(wi_hbm, wi, w_sem.at[0]),
        pltpu.make_async_copy(wo_hbm, wo, w_sem.at[1]),
    ]
    for load in loads:
        load.start()

    mine = core * (M // 2) + x * XB + (zl % NZ) * R
    own = [
        pltpu.make_async_copy(src, xg.at[a * PAIRS + zl // NZ, rows(mine, R)], own_sem.at[a])
        for a, src in enumerate((tok, grad))
    ]
    for copy in own:
        copy.start()

    barrier = pltpu.get_barrier_semaphore()
    for to in xs + zs + [sibling, up, down, far]:
        pl.semaphore_signal(barrier, inc=1, device_id=to, device_id_type=MESH)
    pl.semaphore_wait(barrier, 10)

    def spread_z(a):
        src = (tok, grad)[a]
        dst = xg.at[a * PAIRS + zl // NZ, rows(mine, R)]
        for k in range(3):
            send(src, dst, az_s.at[a, k], az_r.at[a, zl], zs[k])

    def spread_x(i):
        a, p = i // PAIRS, i % PAIRS
        for j in range(NZ):
            source = p * NZ + j
            landed = xg.at[i, rows(core * (M // 2) + x * XB + j * R, R)]

            @pl.when(source != zl)
            def _():
                arrived(landed, az_r.at[a, source])

        block = xg.at[i, rows(core * (M // 2) + x * XB, XB)]
        for k in range(3):
            send(block, block, ax_s.at[i, k], ax_r.at[i, x], xs[k])

    def spread_core(i):
        for k in (1, 2, 3):
            other = ring(x, k)
            arrived(xg.at[i, rows(core * (M // 2) + other * XB, XB)], ax_r.at[i, other])
        half = xg.at[i, rows(core * (M // 2), M // 2)]
        send(half, half, ac_s.at[i], ac_r.at[i], sibling)

    def first_matmul(i):
        arrived(xg.at[i, rows((1 - core) * (M // 2), M // 2)], ac_r.at[i])
        weight = (wi, wot)[i // PAIRS]

        @pl.loop(0, W // TILE)
        def _(n):
            value = jnp.dot(xg[i], weight[:, columns(n)], preferred_element_type=f32)
            part[i, :, columns(n)] = value
            ysend[i, :, columns(n)] = value.astype(bf16)

    def reduce_y_start(i):
        two, one, back = ring(y, 2) * YB, ring(y, 1) * YB, ring(y, 3) * YB
        send(ysend.at[i, rows(two, HB)], yrm.at[i, 0], c_s.at[i, 0], cm_r.at[i, 0], up)
        send(ysend.at[i, rows(two + HB, HB)], yrp.at[i, 0], c_s.at[i, 1], cp_r.at[i, 0], down)
        send(ysend.at[i, rows(one + HB, HB)], yrm.at[i, 2], c_s.at[i, 2], cm_r.at[i, 2], up)
        send(ysend.at[i, rows(back, HB)], yrp.at[i, 2], c_s.at[i, 3], cp_r.at[i, 2], down)

    def reduce_y_middle(i):
        one, back = ring(y, 1) * YB, ring(y, 3) * YB
        arrived(yrm.at[i, 0], cm_r.at[i, 0])
        ycomb[i, 0] = (part[i, rows(one, HB), :] + yrm[i, 0].astype(f32)).astype(bf16)
        send(ycomb.at[i, 0], yrm.at[i, 1], c_s.at[i, 4], cm_r.at[i, 1], up)
        arrived(yrp.at[i, 0], cp_r.at[i, 0])
        ycomb[i, 1] = (part[i, rows(back + HB, HB), :] + yrp[i, 0].astype(f32)).astype(bf16)
        send(ycomb.at[i, 1], yrp.at[i, 1], c_s.at[i, 5], cp_r.at[i, 1], down)

    def reduce_y_end(i):
        for h in (1, 2):
            arrived(yrm.at[i, h], cm_r.at[i, h])
            arrived(yrp.at[i, h], cp_r.at[i, h])
        ysum[i, 0] = part[i, rows(y * YB, HB), :] + yrm[i, 1].astype(f32) + yrp[i, 2].astype(f32)
        ysum[i, 1] = part[i, rows(y * YB + HB, HB), :] + yrm[i, 2].astype(f32) + yrp[i, 1].astype(f32)
        zsend[i] = ysum[i, 1 - zh].astype(bf16)
        send(zsend.at[i], zrecv.at[i], d_s.at[i], d_r.at[i], far)

    def activate(i):
        arrived(zrecv.at[i], d_r.at[i])
        a, p = i // PAIRS, i % PAIRS
        here = rows(y * YB + zh * HB, HB)

        @pl.loop(0, W // TILE)
        def _(n):
            value = ysum[i, zh, :, columns(n)] + zrecv[i, :, columns(n)].astype(f32)
            if a == 0:
                hid[p, :, columns(n)] = value
                inner = tanh_scale * (value + cube_weight * value * value * value)
                result = 0.5 * value * (1.0 + jnp.tanh(inner))
            else:
                h = hid[p, :, columns(n)]
                t = jnp.tanh(tanh_scale * (h + cube_weight * h * h * h))
                slope = 0.5 * (1.0 + t) + 0.5 * h * (1.0 - t * t) * tanh_scale * (
                    1.0 + 3.0 * cube_weight * h * h
                )
                result = value * slope
            ag[i, here, columns(n)] = result.astype(bf16)

        block = ag.at[i, here]
        send(block, block, f_s.at[i], f_r.at[i], far)
        send(block, block, g_s.at[i, 0], gm_r.at[i, 0], up)
        send(block, block, g_s.at[i, 1], gp_r.at[i, 0], down)

    def gather_y_middle(i):
        block = ag.at[i, rows(y * YB + (1 - zh) * HB, HB)]
        arrived(block, f_r.at[i])
        send(block, block, g_s.at[i, 2], gm_r.at[i, 1], up)
        send(block, block, g_s.at[i, 3], gp_r.at[i, 1], down)

    def gather_y_forward(i):
        block = ag.at[i, rows(ring(y, 3) * YB + zh * HB, HB)]
        arrived(block, gm_r.at[i, 0])
        send(block, block, g_s.at[i, 4], gm_r.at[i, 2], up)
        block = ag.at[i, rows(ring(y, 1) * YB + (1 - zh) * HB, HB)]
        arrived(block, gp_r.at[i, 1])
        send(block, block, g_s.at[i, 5], gp_r.at[i, 2], down)

    def second_matmul(i):
        arrived(ag.at[i, rows(ring(y, 3) * YB + (1 - zh) * HB, HB)], gm_r.at[i, 1])
        arrived(ag.at[i, rows(ring(y, 1) * YB + zh * HB, HB)], gp_r.at[i, 0])
        arrived(ag.at[i, rows(ring(y, 2) * YB + zh * HB, HB)], gm_r.at[i, 2])
        arrived(ag.at[i, rows(ring(y, 2) * YB + (1 - zh) * HB, HB)], gp_r.at[i, 2])
        weight = (wo, wit)[i // PAIRS]

        @pl.loop(0, W // TILE)
        def _(n):
            part[i, :, columns(n)] = jnp.dot(
                ag[i], weight[:, columns(n)], preferred_element_type=f32
            )

        send(
            part.at[i, rows((1 - core) * (M // 2), M // 2)], crecv.at[i],
            ic_s.at[i], ic_r.at[i], sibling,
        )

    def reduce_x_start(i):
        arrived(crecv.at[i], ic_r.at[i])

        @pl.loop(0, 4)
        def _(b):
            value = part[i, rows(core * (M // 2) + b * XB, XB), :] + crecv[i, rows(b * XB, XB), :]
            crecv[i, rows(b * XB, XB), :] = value
            xsend[i, rows(b * XB, XB), :] = value.astype(bf16)

        for k in (1, 2, 3):
            block = xsend.at[i, rows(ring(x, k) * XB, XB)]
            send(block, xrecv.at[i, x], ix_s.at[i, k - 1], ix_r.at[i, x], xs[k - 1])

    def reduce_x_end(i):
        for k in (1, 2, 3):
            other = ring(x, k)
            arrived(xrecv.at[i, other], ix_r.at[i, other])
        total = crecv[i, rows(x * XB, XB), :]
        for k in (1, 2, 3):
            total = total + xrecv[i, ring(x, k)].astype(f32)
        a, p = i // PAIRS, i % PAIRS
        for j in range(NZ):
            zrsum[a, p * NZ + j] = total[j * R : (j + 1) * R]
            zosend[a, p * NZ + j] = total[j * R : (j + 1) * R].astype(bf16)

    def reduce_z_start(a):
        for k in (1, 2, 3):
            to = ring(zl, k)
            send(zosend.at[a, to], zorecv.at[a, zl], iz_s.at[a, k - 1], iz_r.at[a, zl], zs[k - 1])

    def reduce_z_end(a):
        for k in (1, 2, 3):
            other = ring(zl, k)
            arrived(zorecv.at[a, other], iz_r.at[a, other])
        total = zrsum[a, zl]
        for k in (1, 2, 3):
            total = total + zorecv[a, ring(zl, k)].astype(f32)
        (out, gout)[a][...] = total.astype(bf16)

    spread_z(0)
    for copy in own:
        copy.wait()
    for load in loads:
        load.wait()

    @pl.loop(0, W // TILE)
    def _(n):
        wot[:, columns(n)] = wo[columns(n), :].T
        wit[:, columns(n)] = wi[columns(n), :].T

    for i in range(PAIRS):
        spread_x(i)
    spread_z(1)
    for i in range(N):
        spread_core(i)
        if i >= 1 and i - 1 + PAIRS < N:
            spread_x(i - 1 + PAIRS)
        first_matmul(i)
        if i >= 1:
            reduce_y_middle(i - 1)
        reduce_y_start(i)
        if i >= 2:
            reduce_y_end(i - 2)
        if i >= 5:
            activate(i - 5)
    reduce_y_middle(N - 1)
    reduce_y_end(N - 2)
    reduce_y_end(N - 1)
    done = max(0, N - 5)
    for i in range(done):
        gather_y_middle(i)
        gather_y_forward(i)
    for i in range(done, N):
        activate(i)
        if i - 2 >= done:
            gather_y_middle(i - 2)
            gather_y_forward(i - 2)
        if i >= done:
            j = i - done
            second_matmul(j)
            if j >= 1:
                reduce_x_start(j - 1)
            if j >= 2:
                reduce_x_end(j - 2)
    for i in range(N - 2, N):
        gather_y_middle(i)
        gather_y_forward(i)
    for j in range(N - done, N):
        second_matmul(j)
        reduce_x_start(j - 1)
        reduce_x_end(j - 2)
        if j - 2 == PAIRS - 1:
            reduce_z_start(0)
    reduce_x_start(N - 1)
    reduce_x_end(N - 2)
    reduce_z_end(0)
    reduce_x_end(N - 1)
    reduce_z_start(1)
    reduce_z_end(1)
    for copy in started:
        copy.wait_send()


def on_device(tokens, weight_in, weight_out, grad_out):
    vmem = pltpu.VMEM
    dma = pltpu.SemaphoreType.DMA
    block = jax.ShapeDtypeStruct((R, W), bf16)
    return pl.pallas_call(
        kernel,
        out_shape=(block, block),
        in_specs=[pl.BlockSpec(memory_space=vmem)] * 2 + [pl.BlockSpec(memory_space=pl.ANY)] * 2,
        out_specs=(pl.BlockSpec(memory_space=vmem),) * 2,
        scratch_shapes=[
            vmem((W, W), bf16),
            vmem((W, W), bf16),
            vmem((W, W), bf16),
            vmem((W, W), bf16),
            vmem((N, M, W), bf16),
            vmem((N, M, W), f32),
            vmem((N, M, W), bf16),
            vmem((N, 3, HB, W), bf16),
            vmem((N, 3, HB, W), bf16),
            vmem((N, 2, HB, W), bf16),
            vmem((N, 2, HB, W), f32),
            vmem((N, HB, W), bf16),
            vmem((N, HB, W), bf16),
            vmem((PAIRS, HB, W), f32),
            vmem((N, M, W), bf16),
            vmem((N, M // 2, W), f32),
            vmem((N, M // 2, W), bf16),
            vmem((N, 4, XB, W), bf16),
            vmem((2, 4, R, W), f32),
            vmem((2, 4, R, W), bf16),
            vmem((2, 4, R, W), bf16),
            dma((2,)), dma((2,)),
            dma((2, 3)), dma((2, 4)),
            dma((N, 3)), dma((N, 4)),
            dma((N,)), dma((N,)),
            dma((N, 6)), dma((N, 3)), dma((N, 3)),
            dma((N,)), dma((N,)),
            dma((N,)), dma((N,)),
            dma((N, 6)), dma((N, 3)), dma((N, 3)),
            dma((N,)), dma((N,)),
            dma((N, 3)), dma((N, 4)),
            dma((2, 3)), dma((2, 4)),
        ],
        compiler_params=pltpu.CompilerParams(
            collective_id=0, has_side_effects=True, vmem_limit_bytes=60 * 1024 * 1024
        ),
        cost_estimate=pl.CostEstimate(
            flops=8 * 512 * W * W, bytes_accessed=4 * W * W, transcendentals=2 * 64 * W
        ),
        name="feed_forward",
    )(tokens, grad_out, weight_in, weight_out)


def solution(mesh):
    placed = (P("row", "col"), P("col", "row"), P("row", "col"), P("row", "col"))
    return jax.shard_map(
        on_device,
        mesh=mesh,
        in_specs=placed,
        out_specs=(P("row", "col"), P("row", "col")),
        check_vma=False,
    )
```

```python
import functools

import jax
import jax.numpy as jnp
from jax import lax
from jax.experimental import pallas as pl
from jax.experimental.pallas import tpu as pltpu
from jax.sharding import PartitionSpec as P

MESH = pl.DeviceIdType.MESH
f32, bf16 = jnp.float32, jnp.bfloat16
tanh_scale = 0.7978845608028654
cube_weight = 0.044715

W = 1536
R = 16
NZ = 1
PAIRS = 4 // NZ
N = 2 * PAIRS
M = 128 * NZ
XB, YB, HB = M // 8, M // 4, M // 8
TILE = 512
ORDER = (
    0, 10, 1, 11, 12, 13, 21, 20, 160, 22, 15, 14, 31, 17, 32, 23, 30, 41,
    51, 16, 42, 24, 33, 25, 52, 161, 61, 26, 27, 43, 53, 40, 62, 50, 35, 34,
    71, 63, 37, 45, 36, 72, 55, 44, 60, 47, 73, 54, 57, 81, 70, 65, 46, 64,
    56, 82, 83, 74, 66, 67, 80, 75, 103, 102, 101, 91, 77, 92, 93, 76, 111, 84,
    112, 90, 85, 113, 87, 122, 110, 100, 105, 86, 121, 94, 132, 104, 120, 95, 123, 114,
    97, 142, 106, 130, 115, 131, 107, 96, 124, 117, 133, 125, 116, 134, 141, 127, 143, 135,
    126, 140, 144, 137, 136, 145, 147, 153, 146, 157,
)


def columns(step):
    return pl.ds(pl.multiple_of(step * TILE, TILE), TILE)


def rows(start, size):
    return pl.ds(pl.multiple_of(start, R), size)


def kernel(
    tok, grad, wi_hbm, wo_hbm, out, gout,
    wi, wo, wit, wot, xg, part, ysend, yrm, yrp, ycomb, ysum, zsend, zrecv, hid, ag,
    crecv, xsend, xrecv, zrsum, zosend, zorecv,
    w_sem, az_s, az_r, ax_s, ax_r, ac_s, ac_r, c_s, cm_r, cp_r, d_s, d_r, f_s, f_r,
    g_s, gm_r, gp_r, ic_s, ic_r, ix_s, ix_r, iz_s, iz_r,
):
    row, col = lax.axis_index("row"), lax.axis_index("col")
    core, x, zl = row % 2, (row // 2) % 4, row // 8
    y, zh = col // 2, col % 2

    def device(x=x, zl=zl, core=core, y=y, zh=zh):
        return ((zl * 4 + x) * 2 + core, y * 2 + zh)

    def ring(i, k):
        return (i + k) % 4

    xs = [device(x=ring(x, k)) for k in (1, 2, 3)]
    zs = [device(zl=ring(zl, k)) for k in (1, 2, 3)]
    sibling = device(core=1 - core)
    up, down = device(y=ring(y, 1)), device(y=ring(y, 3))
    far = device(zh=1 - zh)

    def send(src, dst, s_sem, r_sem, to):
        copy = pltpu.make_async_remote_copy(
            src_ref=src, dst_ref=dst, send_sem=s_sem, recv_sem=r_sem,
            device_id=to, device_id_type=MESH,
        )
        copy.start()

    def arrived(ref, sem):
        pltpu.make_async_copy(ref, ref, sem).wait()

    loads = [
        pltpu.make_async_copy(wi_hbm, wi, w_sem.at[0]),
        pltpu.make_async_copy(wo_hbm, wo, w_sem.at[1]),
    ]
    for load in loads:
        load.start()

    waited = set()

    def loaded(k):
        if k not in waited:
            waited.add(k)
            loads[k].wait()

    mine = core * (M // 2) + x * XB + (zl % NZ) * R
    for a, src in enumerate((tok, grad)):
        xg[a * PAIRS + zl // NZ, rows(mine, R), :] = src[...]

    barrier = pltpu.get_barrier_semaphore()
    for to in xs + zs + [sibling, up, down, far]:
        pl.semaphore_signal(barrier, inc=1, device_id=to, device_id_type=MESH)
    pl.semaphore_wait(barrier, 10)

    def spread_z(a):
        src = (tok, grad)[a]
        dst = xg.at[a * PAIRS + zl // NZ, rows(mine, R)]
        for k in range(3):
            send(src, dst, az_s, az_r.at[a, zl], zs[k])

    def spread_x(i):
        a, p = i // PAIRS, i % PAIRS
        for j in range(NZ):
            source = p * NZ + j
            landed = xg.at[i, rows(core * (M // 2) + x * XB + j * R, R)]

            @pl.when(source != zl)
            def _():
                arrived(landed, az_r.at[a, source])

        block = xg.at[i, rows(core * (M // 2) + x * XB, XB)]
        send(block, block, ax_s, ax_r.at[i, 0], xs[0])
        send(block, block, ax_s, ax_r.at[i, 1], xs[2])

    def forward_x(i):
        k = i % 2
        block = xg.at[i, rows(core * (M // 2) + ring(x, 3 - 2 * k) * XB, XB)]
        arrived(block, ax_r.at[i, k])
        send(block, block, ax_s, ax_r.at[i, 2], xs[2 * k])

    def spread_core(i):
        k = 1 - i % 2
        arrived(xg.at[i, rows(core * (M // 2) + ring(x, 3 - 2 * k) * XB, XB)], ax_r.at[i, k])
        arrived(xg.at[i, rows(core * (M // 2) + ring(x, 2) * XB, XB)], ax_r.at[i, 2])
        half = xg.at[i, rows(core * (M // 2), M // 2)]
        send(half, half, ac_s, ac_r.at[i], sibling)

    def first_matmul(i):
        arrived(xg.at[i, rows((1 - core) * (M // 2), M // 2)], ac_r.at[i])
        weight = (wi, wot)[i // PAIRS]
        loaded(i // PAIRS)

        @pl.loop(0, W // TILE)
        def _(n):
            value = jnp.dot(xg[i], weight[:, columns(n)], preferred_element_type=f32)
            part[i, :, columns(n)] = value
            ysend[i, :, columns(n)] = value.astype(bf16)

    def reduce_y_start(i):
        two, one, back = ring(y, 2) * YB, ring(y, 1) * YB, ring(y, 3) * YB
        send(ysend.at[i, rows(two, HB)], yrm.at[i, 0], c_s, cm_r.at[i, 0], up)
        send(ysend.at[i, rows(two + HB, HB)], yrp.at[i, 0], c_s, cp_r.at[i, 0], down)
        send(ysend.at[i, rows(one + HB, HB)], yrm.at[i, 2], c_s, cm_r.at[i, 2], up)
        send(ysend.at[i, rows(back, HB)], yrp.at[i, 2], c_s, cp_r.at[i, 2], down)

    def reduce_y_middle(i):
        one, back = ring(y, 1) * YB, ring(y, 3) * YB
        arrived(yrm.at[i, 0], cm_r.at[i, 0])
        ycomb[i, 0] = (part[i, rows(one, HB), :] + yrm[i, 0].astype(f32)).astype(bf16)
        send(ycomb.at[i, 0], yrm.at[i, 1], c_s, cm_r.at[i, 1], up)
        arrived(yrp.at[i, 0], cp_r.at[i, 0])
        ycomb[i, 1] = (part[i, rows(back + HB, HB), :] + yrp[i, 0].astype(f32)).astype(bf16)
        send(ycomb.at[i, 1], yrp.at[i, 1], c_s, cp_r.at[i, 1], down)

    def reduce_y_end(i):
        for h in (1, 2):
            arrived(yrm.at[i, h], cm_r.at[i, h])
            arrived(yrp.at[i, h], cp_r.at[i, h])
        ysum[i, 0] = part[i, rows(y * YB, HB), :] + yrm[i, 1].astype(f32) + yrp[i, 2].astype(f32)
        ysum[i, 1] = part[i, rows(y * YB + HB, HB), :] + yrm[i, 2].astype(f32) + yrp[i, 1].astype(f32)
        zsend[i] = ysum[i, 1 - zh].astype(bf16)
        send(zsend.at[i], zrecv.at[i], d_s, d_r.at[i], far)

    def activate(i):
        arrived(zrecv.at[i], d_r.at[i])
        a, p = i // PAIRS, i % PAIRS
        here = rows(y * YB + zh * HB, HB)

        @pl.loop(0, W // TILE)
        def _(n):
            value = ysum[i, zh, :, columns(n)] + zrecv[i, :, columns(n)].astype(f32)
            if a == 0:
                hid[p, :, columns(n)] = value
                inner = tanh_scale * (value + cube_weight * value * value * value)
                result = 0.5 * value * (1.0 + jnp.tanh(inner))
            else:
                h = hid[p, :, columns(n)]
                t = jnp.tanh(tanh_scale * (h + cube_weight * h * h * h))
                slope = 0.5 * (1.0 + t) + 0.5 * h * (1.0 - t * t) * tanh_scale * (
                    1.0 + 3.0 * cube_weight * h * h
                )
                result = value * slope
            ag[i, here, columns(n)] = result.astype(bf16)

        block = ag.at[i, here]
        send(block, block, f_s, f_r.at[i], far)
        send(block, block, g_s, gm_r.at[i, 0], up)
        send(block, block, g_s, gp_r.at[i, 0], down)

    def gather_y_middle(i):
        block = ag.at[i, rows(y * YB + (1 - zh) * HB, HB)]
        arrived(block, f_r.at[i])
        send(block, block, g_s, gm_r.at[i, 1], up)
        send(block, block, g_s, gp_r.at[i, 1], down)

    def gather_y_up(i):
        block = ag.at[i, rows(ring(y, 3) * YB + zh * HB, HB)]
        arrived(block, gm_r.at[i, 0])
        send(block, block, g_s, gm_r.at[i, 2], up)

    def gather_y_down(i):
        block = ag.at[i, rows(ring(y, 1) * YB + (1 - zh) * HB, HB)]
        arrived(block, gp_r.at[i, 1])
        send(block, block, g_s, gp_r.at[i, 2], down)

    def second_matmul(i):
        arrived(ag.at[i, rows(ring(y, 3) * YB + (1 - zh) * HB, HB)], gm_r.at[i, 1])
        arrived(ag.at[i, rows(ring(y, 1) * YB + zh * HB, HB)], gp_r.at[i, 0])
        arrived(ag.at[i, rows(ring(y, 2) * YB + zh * HB, HB)], gm_r.at[i, 2])
        arrived(ag.at[i, rows(ring(y, 2) * YB + (1 - zh) * HB, HB)], gp_r.at[i, 2])
        weight = (wo, wit)[i // PAIRS]

        @pl.loop(0, W // TILE)
        def _(n):
            part[i, :, columns(n)] = jnp.dot(
                ag[i], weight[:, columns(n)], preferred_element_type=f32
            )

        send(
            part.at[i, rows((1 - core) * (M // 2), M // 2)], crecv.at[i],
            ic_s, ic_r.at[i], sibling,
        )

    def reduce_x_start(i):
        arrived(crecv.at[i], ic_r.at[i])

        @pl.loop(0, 4)
        def _(b):
            value = part[i, rows(core * (M // 2) + b * XB, XB), :] + crecv[i, rows(b * XB, XB), :]
            crecv[i, rows(b * XB, XB), :] = value
            xsend[i, rows(b * XB, XB), :] = value.astype(bf16)

        for k in (1, 2, 3):
            block = xsend.at[i, rows(ring(x, k) * XB, XB)]
            send(block, xrecv.at[i, x], ix_s, ix_r.at[i, x], xs[k - 1])

    def reduce_x_end(i):
        for k in (1, 2, 3):
            other = ring(x, k)
            arrived(xrecv.at[i, other], ix_r.at[i, other])
        total = crecv[i, rows(x * XB, XB), :]
        for k in (1, 2, 3):
            total = total + xrecv[i, ring(x, k)].astype(f32)
        a, p = i // PAIRS, i % PAIRS
        for j in range(NZ):
            owner = p * NZ + j
            piece = total[j * R : (j + 1) * R]
            zrsum[a, owner] = piece
            zosend[a, owner] = piece.astype(bf16)

            @pl.when(zl != owner)
            def _():
                pltpu.make_async_remote_copy(
                    src_ref=zosend.at[a, owner], dst_ref=zorecv.at[a, zl],
                    send_sem=iz_s, recv_sem=iz_r.at[a, zl],
                    device_id=device(zl=owner), device_id_type=MESH,
                ).start()

    def reduce_z_end(a):
        for k in (1, 2, 3):
            other = ring(zl, k)
            arrived(zorecv.at[a, other], iz_r.at[a, other])
        total = zrsum[a, zl]
        for k in (1, 2, 3):
            total = total + zorecv[a, ring(zl, k)].astype(f32)
        (out, gout)[a][...] = total.astype(bf16)

    def turn_out():
        loaded(1)

        @pl.loop(0, W // TILE)
        def _(n):
            wot[:, columns(n)] = wo[columns(n), :].T

    def turn_in():
        loaded(0)

        @pl.loop(0, W // TILE)
        def _(n):
            wit[:, columns(n)] = wi[columns(n), :].T

    def reduce_z(i):
        if i % PAIRS == PAIRS - 1:
            reduce_z_end(i // PAIRS)

    def turn(k):
        (turn_out, turn_in)[k]()

    stages = (
        spread_z, spread_x, forward_x, spread_core, first_matmul,
        reduce_y_start, reduce_y_middle, reduce_y_end, activate,
        gather_y_middle, gather_y_up, gather_y_down,
        second_matmul, reduce_x_start, reduce_x_end, reduce_z, turn,
    )
    for code in ORDER:
        stages[code // 10](code % 10)
    for sem, ref in (
        (az_s, xg.at[0, pl.ds(0, 6 * R)]),
        (ax_s, xg.at[pl.ds(0, 3)]),
        (ac_s, xg.at[pl.ds(0, 4)]),
        (c_s, xg.at[pl.ds(0, 6)]),
        (d_s, xg.at[0]),
        (f_s, xg.at[0]),
        (g_s, xg.at[pl.ds(0, 6)]),
        (ic_s, crecv),
        (ix_s, xg.at[pl.ds(0, 3)]),
        (iz_s, xg.at[0, pl.ds(0, 6 * R)]),
    ):
        arrived(ref, sem)


def on_device(tokens, weight_in, weight_out, grad_out):
    vmem = pltpu.VMEM
    dma = pltpu.SemaphoreType.DMA
    block = jax.ShapeDtypeStruct((R, W), bf16)
    return pl.pallas_call(
        kernel,
        out_shape=(block, block),
        in_specs=[pl.BlockSpec(memory_space=vmem)] * 2 + [pl.BlockSpec(memory_space=pl.ANY)] * 2,
        out_specs=(pl.BlockSpec(memory_space=vmem),) * 2,
        scratch_shapes=[
            vmem((W, W), bf16),
            vmem((W, W), bf16),
            vmem((W, W), bf16),
            vmem((W, W), bf16),
            vmem((N, M, W), bf16),
            vmem((N, M, W), f32),
            vmem((N, M, W), bf16),
            vmem((N, 3, HB, W), bf16),
            vmem((N, 3, HB, W), bf16),
            vmem((N, 2, HB, W), bf16),
            vmem((N, 2, HB, W), f32),
            vmem((N, HB, W), bf16),
            vmem((N, HB, W), bf16),
            vmem((PAIRS, HB, W), f32),
            vmem((N, M, W), bf16),
            vmem((N, M // 2, W), f32),
            vmem((N, M // 2, W), bf16),
            vmem((N, 4, XB, W), bf16),
            vmem((2, 4, R, W), f32),
            vmem((2, 4, R, W), bf16),
            vmem((2, 4, R, W), bf16),
            dma((2,)),
            dma, dma((2, 4)),
            dma, dma((N, 3)),
            dma, dma((N,)),
            dma, dma((N, 3)), dma((N, 3)),
            dma, dma((N,)),
            dma, dma((N,)),
            dma, dma((N, 3)), dma((N, 3)),
            dma, dma((N,)),
            dma, dma((N, 4)),
            dma, dma((2, 4)),
        ],
        compiler_params=pltpu.CompilerParams(
            collective_id=0, has_side_effects=True, vmem_limit_bytes=60 * 1024 * 1024
        ),
        cost_estimate=pl.CostEstimate(
            flops=8 * 512 * W * W, bytes_accessed=4 * W * W, transcendentals=2 * 64 * W
        ),
        name="feed_forward",
    )(tokens, grad_out, weight_in, weight_out)


def solution(mesh):
    placed = (P("row", "col"), P("col", "row"), P("row", "col"), P("row", "col"))
    return jax.shard_map(
        on_device,
        mesh=mesh,
        in_specs=placed,
        out_specs=(P("row", "col"), P("row", "col")),
        check_vma=False,
    )
```

```python
import functools

import jax
import jax.numpy as jnp
from jax import lax
from jax.experimental import pallas as pl
from jax.experimental.pallas import tpu as pltpu
from jax.sharding import PartitionSpec as P

MESH = pl.DeviceIdType.MESH
f32, bf16 = jnp.float32, jnp.bfloat16
tanh_scale = 0.7978845608028654
cube_weight = 0.044715

W = 1536
R = 16
PAIRS = 4
N = 2 * PAIRS
M = 128
XB, YB, HB = M // 8, M // 4, M // 8
DIRECT = ()
TILE = 512
ORDER = (
    1, 10, 7, 3, 14, 2, 20, 11, 24, 5, 160, 30, 6, 21, 17, 34, 40, 13,
    50, 31, 27, 44, 54, 12, 41, 23, 60, 51, 16, 15, 37, 22, 64, 47, 70, 33,
    57, 26, 25, 32, 61, 43, 53, 74, 35, 67, 42, 71, 52, 36, 45, 63, 55, 80,
    46, 77, 73, 62, 65, 56, 81, 72, 75, 90, 66, 83, 110, 161, 76, 87, 84, 91,
    101, 82, 107, 100, 103, 93, 111, 86, 85, 113, 121, 97, 94, 120, 92, 123, 117, 96,
    102, 131, 112, 106, 130, 95, 105, 127, 116, 114, 133, 104, 122, 115, 141, 137, 126, 140,
    132, 143, 125, 147, 136, 124, 142, 135, 146, 134, 145, 150, 144, 151,
)


def columns(step):
    return pl.ds(pl.multiple_of(step * TILE, TILE), TILE)


def rows(start, size):
    return pl.ds(pl.multiple_of(start, R), size)


def kernel(
    tok, grad, wi_hbm, wo_hbm, out,
    wi, wo, wit, wot, xg, part, ysend, yrm, yrp, ycomb, ysum, zsend, zrecv, hid, ag,
    crecv, xsend, xrecv, zrsum, zosend, zorecv,
    w_sem, az_s, az_r, ax_s, ax_r, ac_s, ac_r, c_s, cm_r, cp_r, d_s, d_r, f_s, f_r,
    g_s, gm_r, gp_r, ic_s, ic_r, ix_s, ix_r, iz_s, iz_r,
):
    row, col = lax.axis_index("row"), lax.axis_index("col")
    core, x, zl = row % 2, (row // 2) % 4, row // 8
    y, zh = col // 2, col % 2

    def device(x=x, zl=zl, core=core, y=y, zh=zh):
        return ((zl * 4 + x) * 2 + core, y * 2 + zh)

    def ring(i, k):
        return (i + k) % 4

    xs = [device(x=ring(x, k)) for k in (1, 2, 3)]
    zs = [
        device(zl=plane)
        for plane in (zl + 1 - 2 * (zl % 2), zl + 2 - 4 * (zl // 2), 3 - zl)
    ]
    sibling = device(core=1 - core)
    up, down = device(y=ring(y, 1)), device(y=ring(y, 3))
    far = device(zh=1 - zh)

    def send(src, dst, s_sem, r_sem, to):
        copy = pltpu.make_async_remote_copy(
            src_ref=src, dst_ref=dst, send_sem=s_sem, recv_sem=r_sem,
            device_id=to, device_id_type=MESH,
        )
        copy.start()

    def arrived(ref, sem):
        pltpu.make_async_copy(ref, ref, sem).wait()

    loads = [
        pltpu.make_async_copy(wi_hbm, wi, w_sem.at[0]),
        pltpu.make_async_copy(wo_hbm, wo, w_sem.at[1]),
    ]
    for load in loads:
        load.start()

    waited = set()

    def loaded(k):
        if k not in waited:
            waited.add(k)
            loads[k].wait()

    mine = rows(core * (M // 2) + x * XB, XB)
    for a, src in enumerate((tok, grad)):
        xg[a * PAIRS, mine, :] = src[...]

    barrier = pltpu.get_barrier_semaphore()
    for to in xs + zs + [sibling, up, down, far]:
        pl.semaphore_signal(barrier, inc=1, device_id=to, device_id_type=MESH)
    pl.semaphore_wait(barrier, 10)

    def spread_z(i):
        a, k = i // PAIRS, i % PAIRS
        send((tok, grad)[a], xg.at[i, mine], az_s, az_r.at[a, k], zs[k - 1])

    def spread_x(i):
        a, k = i // PAIRS, i % PAIRS
        block = xg.at[i, mine]
        if k > 0:
            arrived(block, az_r.at[a, k])
        send(block, block, ax_s, ax_r.at[i, 0], xs[0])
        send(block, block, ax_s, ax_r.at[i, 1], xs[2])
        if i in DIRECT:
            send(block, block, ax_s, ax_r.at[i, 2], xs[1])

    def forward_x(i):
        if i in DIRECT:
            return
        k = i % 2
        block = xg.at[i, rows(core * (M // 2) + ring(x, 3 - 2 * k) * XB, XB)]
        arrived(block, ax_r.at[i, k])
        send(block, block, ax_s, ax_r.at[i, 2], xs[2 * k])

    def spread_core(i):
        for k in (0, 1) if i in DIRECT else (1 - i % 2,):
            arrived(xg.at[i, rows(core * (M // 2) + ring(x, 3 - 2 * k) * XB, XB)], ax_r.at[i, k])
        arrived(xg.at[i, rows(core * (M // 2) + ring(x, 2) * XB, XB)], ax_r.at[i, 2])
        half = xg.at[i, rows(core * (M // 2), M // 2)]
        send(half, half, ac_s, ac_r.at[i], sibling)

    def first_matmul(i):
        arrived(xg.at[i, rows((1 - core) * (M // 2), M // 2)], ac_r.at[i])
        weight = (wi, wot)[i // PAIRS]
        loaded(i // PAIRS)

        @pl.loop(0, W // TILE)
        def _(n):
            value = jnp.dot(xg[i], weight[:, columns(n)], preferred_element_type=f32)
            part[i, :, columns(n)] = value
            ysend[i, :, columns(n)] = value.astype(bf16)

    def reduce_y_start(i):
        two, one, back = ring(y, 2) * YB, ring(y, 1) * YB, ring(y, 3) * YB
        send(ysend.at[i, rows(two, HB)], yrm.at[i, 0], c_s, cm_r.at[i, 0], up)
        send(ysend.at[i, rows(two + HB, HB)], yrp.at[i, 0], c_s, cp_r.at[i, 0], down)
        send(ysend.at[i, rows(one + HB, HB)], yrm.at[i, 2], c_s, cm_r.at[i, 2], up)
        send(ysend.at[i, rows(back, HB)], yrp.at[i, 2], c_s, cp_r.at[i, 2], down)

    def reduce_y_middle(i):
        one, back = ring(y, 1) * YB, ring(y, 3) * YB
        arrived(yrm.at[i, 0], cm_r.at[i, 0])
        ycomb[i, 0] = (part[i, rows(one, HB), :] + yrm[i, 0].astype(f32)).astype(bf16)
        send(ycomb.at[i, 0], yrm.at[i, 1], c_s, cm_r.at[i, 1], up)
        arrived(yrp.at[i, 0], cp_r.at[i, 0])
        ycomb[i, 1] = (part[i, rows(back + HB, HB), :] + yrp[i, 0].astype(f32)).astype(bf16)
        send(ycomb.at[i, 1], yrp.at[i, 1], c_s, cp_r.at[i, 1], down)

    def reduce_y_end(i):
        for h in (1, 2):
            arrived(yrm.at[i, h], cm_r.at[i, h])
            arrived(yrp.at[i, h], cp_r.at[i, h])
        ysum[i, 0] = part[i, rows(y * YB, HB), :] + yrm[i, 1].astype(f32) + yrp[i, 2].astype(f32)
        ysum[i, 1] = part[i, rows(y * YB + HB, HB), :] + yrm[i, 2].astype(f32) + yrp[i, 1].astype(f32)
        zsend[i] = ysum[i, 1 - zh].astype(bf16)
        send(zsend.at[i], zrecv.at[i], d_s, d_r.at[i], far)

    def activate(i):
        arrived(zrecv.at[i], d_r.at[i])
        a, p = i // PAIRS, i % PAIRS
        here = rows(y * YB + zh * HB, HB)

        @pl.loop(0, W // TILE)
        def _(n):
            value = ysum[i, zh, :, columns(n)] + zrecv[i, :, columns(n)].astype(f32)
            if a == 0:
                hid[p, :, columns(n)] = value
                inner = tanh_scale * (value + cube_weight * value * value * value)
                result = 0.5 * value * (1.0 + jnp.tanh(inner))
            else:
                h = hid[p, :, columns(n)]
                t = jnp.tanh(tanh_scale * (h + cube_weight * h * h * h))
                slope = 0.5 * (1.0 + t) + 0.5 * h * (1.0 - t * t) * tanh_scale * (
                    1.0 + 3.0 * cube_weight * h * h
                )
                result = value * slope
            ag[i, here, columns(n)] = result.astype(bf16)

        block = ag.at[i, here]
        send(block, block, f_s, f_r.at[i], far)
        send(block, block, g_s, gm_r.at[i, 0], up)
        send(block, block, g_s, gp_r.at[i, 0], down)

    def gather_y_middle(i):
        block = ag.at[i, rows(y * YB + (1 - zh) * HB, HB)]
        arrived(block, f_r.at[i])
        send(block, block, g_s, gm_r.at[i, 1], up)
        send(block, block, g_s, gp_r.at[i, 1], down)

    def gather_y_up(i):
        block = ag.at[i, rows(ring(y, 3) * YB + zh * HB, HB)]
        arrived(block, gm_r.at[i, 0])
        send(block, block, g_s, gm_r.at[i, 2], up)

    def gather_y_down(i):
        block = ag.at[i, rows(ring(y, 1) * YB + (1 - zh) * HB, HB)]
        arrived(block, gp_r.at[i, 1])
        send(block, block, g_s, gp_r.at[i, 2], down)

    def second_matmul(i):
        arrived(ag.at[i, rows(ring(y, 3) * YB + (1 - zh) * HB, HB)], gm_r.at[i, 1])
        arrived(ag.at[i, rows(ring(y, 1) * YB + zh * HB, HB)], gp_r.at[i, 0])
        arrived(ag.at[i, rows(ring(y, 2) * YB + zh * HB, HB)], gm_r.at[i, 2])
        arrived(ag.at[i, rows(ring(y, 2) * YB + (1 - zh) * HB, HB)], gp_r.at[i, 2])
        weight = (wo, wit)[i // PAIRS]

        @pl.loop(0, W // TILE)
        def _(n):
            part[i, :, columns(n)] = jnp.dot(
                ag[i], weight[:, columns(n)], preferred_element_type=f32
            )

        send(
            part.at[i, rows((1 - core) * (M // 2), M // 2)], crecv.at[i],
            ic_s, ic_r.at[i], sibling,
        )

    def reduce_x_start(i):
        arrived(crecv.at[i], ic_r.at[i])

        @pl.loop(0, 4)
        def _(b):
            value = part[i, rows(core * (M // 2) + b * XB, XB), :] + crecv[i, rows(b * XB, XB), :]
            crecv[i, rows(b * XB, XB), :] = value
            xsend[i, rows(b * XB, XB), :] = value.astype(bf16)

        for k in (1, 2, 3):
            block = xsend.at[i, rows(ring(x, k) * XB, XB)]
            send(block, xrecv.at[i, x], ix_s, ix_r.at[i, x], xs[k - 1])

    def reduce_x_end(i):
        for k in (1, 2, 3):
            other = ring(x, k)
            arrived(xrecv.at[i, other], ix_r.at[i, other])
        total = crecv[i, rows(x * XB, XB), :]
        for k in (1, 2, 3):
            total = total + xrecv[i, ring(x, k)].astype(f32)
        a, k = i // PAIRS, i % PAIRS
        if k == 0:
            zrsum[a] = total
        else:
            zosend[a, k] = total.astype(bf16)
            send(zosend.at[a, k], zorecv.at[a, k], iz_s, iz_r.at[a, k], zs[k - 1])

    def reduce_z(a):
        total = zrsum[a]
        for k in (1, 2, 3):
            arrived(zorecv.at[a, k], iz_r.at[a, k])
            total = total + zorecv[a, k].astype(f32)
        out[a] = total.astype(bf16)

    def turn_out():
        loaded(1)

        @pl.loop(0, W // TILE)
        def _(n):
            wot[:, columns(n)] = wo[columns(n), :].T

    def turn_in():
        loaded(0)

        @pl.loop(0, W // TILE)
        def _(n):
            wit[:, columns(n)] = wi[columns(n), :].T

    def turn(k):
        (turn_out, turn_in)[k]()

    stages = (
        spread_z, spread_x, forward_x, spread_core, first_matmul,
        reduce_y_start, reduce_y_middle, reduce_y_end, activate,
        gather_y_middle, gather_y_up, gather_y_down,
        second_matmul, reduce_x_start, reduce_x_end, reduce_z, turn,
    )
    for code in ORDER:
        stages[code // 10](code % 10)
    for sem, ref in (
        (az_s, xg.at[0, pl.ds(0, 6 * R)]),
        (ax_s, xg.at[pl.ds(0, 3)]),
        (ac_s, xg.at[pl.ds(0, 4)]),
        (c_s, xg.at[pl.ds(0, 6)]),
        (d_s, xg.at[0]),
        (f_s, xg.at[0]),
        (g_s, xg.at[pl.ds(0, 6)]),
        (ic_s, crecv),
        (ix_s, xg.at[pl.ds(0, 3)]),
        (iz_s, xg.at[0, pl.ds(0, 6 * R)]),
    ):
        arrived(ref, sem)


def on_device(tokens, weight_in, weight_out, grad_out):
    vmem = pltpu.VMEM
    dma = pltpu.SemaphoreType.DMA
    block = jax.ShapeDtypeStruct((2, R, W), bf16)
    both = pl.pallas_call(
        kernel,
        out_shape=block,
        in_specs=[pl.BlockSpec(memory_space=vmem)] * 2 + [pl.BlockSpec(memory_space=pl.ANY)] * 2,
        out_specs=pl.BlockSpec(memory_space=vmem),
        scratch_shapes=[
            vmem((W, W), bf16),
            vmem((W, W), bf16),
            vmem((W, W), bf16),
            vmem((W, W), bf16),
            vmem((N, M, W), bf16),
            vmem((N, M, W), f32),
            vmem((N, M, W), bf16),
            vmem((N, 3, HB, W), bf16),
            vmem((N, 3, HB, W), bf16),
            vmem((N, 2, HB, W), bf16),
            vmem((N, 2, HB, W), f32),
            vmem((N, HB, W), bf16),
            vmem((N, HB, W), bf16),
            vmem((PAIRS, HB, W), f32),
            vmem((N, M, W), bf16),
            vmem((N, M // 2, W), f32),
            vmem((N, M // 2, W), bf16),
            vmem((N, 4, XB, W), bf16),
            vmem((2, R, W), f32),
            vmem((2, 4, R, W), bf16),
            vmem((2, 4, R, W), bf16),
            dma((2,)),
            dma, dma((2, 4)),
            dma, dma((N, 3)),
            dma, dma((N,)),
            dma, dma((N, 3)), dma((N, 3)),
            dma, dma((N,)),
            dma, dma((N,)),
            dma, dma((N, 3)), dma((N, 3)),
            dma, dma((N,)),
            dma, dma((N, 4)),
            dma, dma((2, 4)),
        ],
        compiler_params=pltpu.CompilerParams(
            collective_id=0, has_side_effects=True, vmem_limit_bytes=60 * 1024 * 1024
        ),
        cost_estimate=pl.CostEstimate(
            flops=8 * 512 * W * W, bytes_accessed=4 * W * W, transcendentals=2 * 64 * W
        ),
        name="feed_forward",
    )(tokens, grad_out, weight_in, weight_out)
    return both[0].astype(bf16), both[1].astype(bf16)


def solution(mesh):
    placed = (P("row", "col"), P("col", "row"), P("row", "col"), P("row", "col"))
    return jax.shard_map(
        on_device,
        mesh=mesh,
        in_specs=placed,
        out_specs=(P("row", "col"), P("row", "col")),
        check_vma=False,
    )
```

```python
import functools

import jax
import jax.numpy as jnp
from jax import lax
from jax.experimental import pallas as pl
from jax.experimental.pallas import tpu as pltpu
from jax.sharding import PartitionSpec as P

MESH = pl.DeviceIdType.MESH
f32, bf16 = jnp.float32, jnp.bfloat16
tanh_scale = 0.7978845608028654
cube_weight = 0.044715

W = 1536
R = 16
PAIRS = 4
N = 2 * PAIRS
M = 128
XB, YB, HB = M // 8, M // 4, M // 8
DIRECT = (0,)
TILE = 512
ORDER = (
    1, 2, 14, 3, 10, 24, 7, 160, 12, 30, 11, 34, 6, 40, 22, 50, 13, 17,
    21, 44, 54, 5, 32, 60, 23, 42, 52, 27, 33, 64, 70, 15, 62, 16, 37, 43,
    31, 53, 74, 47, 25, 57, 72, 26, 41, 161, 63, 51, 36, 80, 67, 73, 35, 61,
    46, 56, 82, 77, 45, 71, 66, 55, 83, 76, 65, 92, 102, 90, 100, 87, 75, 112,
    110, 93, 81, 86, 120, 113, 103, 97, 85, 122, 84, 101, 107, 123, 91, 117, 96, 132,
    105, 111, 133, 106, 130, 104, 95, 127, 116, 94, 121, 142, 115, 137, 126, 114, 143, 131,
    125, 136, 147, 124, 135, 20, 140, 146, 134, 141, 145, 150, 144, 151,
)


def columns(step):
    return pl.ds(pl.multiple_of(step * TILE, TILE), TILE)


def rows(start, size):
    return pl.ds(pl.multiple_of(start, R), size)


def kernel(
    tok, grad, wi_hbm, wo_hbm, out,
    wi, wo, wit, wot, xg, part, ysend, yrm, yrp, ycomb, ysum, zsend, zrecv, hid, ag,
    crecv, xsend, xrecv, zrsum, zosend, zorecv,
    w_sem, own_sem, az_s, az_r, ax_s, ax_r, ac_s, ac_r, c_s, cm_r, cp_r, d_s, d_r, f_s, f_r,
    g_s, gm_r, gp_r, ic_s, ic_r, ix_s, ix_r, iz_s, iz_r,
):
    row, col = lax.axis_index("row"), lax.axis_index("col")
    core, x, zl = row % 2, (row // 2) % 4, row // 8
    y, zh = col // 2, col % 2

    def device(x=x, zl=zl, core=core, y=y, zh=zh):
        return ((zl * 4 + x) * 2 + core, y * 2 + zh)

    def ring(i, k):
        return (i + k) % 4

    xs = [device(x=ring(x, k)) for k in (1, 2, 3)]
    zs = [
        device(zl=plane)
        for plane in (zl + 1 - 2 * (zl % 2), zl + 2 - 4 * (zl // 2), 3 - zl)
    ]
    sibling = device(core=1 - core)
    up, down = device(y=ring(y, 1)), device(y=ring(y, 3))
    far = device(zh=1 - zh)

    def send(src, dst, s_sem, r_sem, to):
        copy = pltpu.make_async_remote_copy(
            src_ref=src, dst_ref=dst, send_sem=s_sem, recv_sem=r_sem,
            device_id=to, device_id_type=MESH,
        )
        copy.start()

    def arrived(ref, sem):
        pltpu.make_async_copy(ref, ref, sem).wait()

    waited = set()

    def loaded(k):
        if k not in waited:
            waited.add(k)
            loads[k].wait()

    mine = rows(core * (M // 2) + x * XB, XB)
    barrier = pltpu.get_barrier_semaphore()
    for to in [far] + zs + xs + [up, down, sibling]:
        pl.semaphore_signal(barrier, inc=1, device_id=to, device_id_type=MESH)
    own = [
        pltpu.make_async_copy(src, xg.at[a * PAIRS, mine], own_sem.at[a])
        for a, src in enumerate((tok, grad))
    ]
    for copy in own:
        copy.start()
    loads = [
        pltpu.make_async_copy(wi_hbm, wi, w_sem.at[0]),
        pltpu.make_async_copy(wo_hbm, wo, w_sem.at[1]),
    ]
    for load in loads:
        load.start()
    for copy in own:
        copy.wait()
    pl.semaphore_wait(barrier, 10)

    def spread_z(i):
        a, k = i // PAIRS, i % PAIRS
        send(xg.at[a * PAIRS, mine], xg.at[i, mine], az_s, az_r.at[a, k], zs[k - 1])

    def spread_x(i):
        a, k = i // PAIRS, i % PAIRS
        block = xg.at[i, mine]
        if k > 0:
            arrived(block, az_r.at[a, k])
        send(block, block, ax_s, ax_r.at[i, 0], xs[0])
        send(block, block, ax_s, ax_r.at[i, 1], xs[2])
        if i in DIRECT:
            send(block, block, ax_s, ax_r.at[i, 2], xs[1])

    def forward_x(i):
        if i in DIRECT:
            return
        k = i % 2
        block = xg.at[i, rows(core * (M // 2) + ring(x, 3 - 2 * k) * XB, XB)]
        arrived(block, ax_r.at[i, k])
        send(block, block, ax_s, ax_r.at[i, 2], xs[2 * k])

    def spread_core(i):
        for k in (0, 1) if i in DIRECT else (1 - i % 2,):
            arrived(xg.at[i, rows(core * (M // 2) + ring(x, 3 - 2 * k) * XB, XB)], ax_r.at[i, k])
        arrived(xg.at[i, rows(core * (M // 2) + ring(x, 2) * XB, XB)], ax_r.at[i, 2])
        half = xg.at[i, rows(core * (M // 2), M // 2)]
        send(half, half, ac_s, ac_r.at[i], sibling)

    def first_matmul(i):
        arrived(xg.at[i, rows((1 - core) * (M // 2), M // 2)], ac_r.at[i])
        weight = (wi, wot)[i // PAIRS]
        loaded(i // PAIRS)

        value = jnp.dot(xg[i], weight[...], preferred_element_type=f32)
        part[i] = value
        ysend[i] = value.astype(bf16)

    def reduce_y_start(i):
        two, one, back = ring(y, 2) * YB, ring(y, 1) * YB, ring(y, 3) * YB
        send(ysend.at[i, rows(two, HB)], yrm.at[i, 0], c_s, cm_r.at[i, 0], up)
        send(ysend.at[i, rows(two + HB, HB)], yrp.at[i, 0], c_s, cp_r.at[i, 0], down)
        send(ysend.at[i, rows(one + HB, HB)], yrm.at[i, 2], c_s, cm_r.at[i, 2], up)
        send(ysend.at[i, rows(back, HB)], yrp.at[i, 2], c_s, cp_r.at[i, 2], down)

    def reduce_y_middle(i):
        one, back = ring(y, 1) * YB, ring(y, 3) * YB
        arrived(yrm.at[i, 0], cm_r.at[i, 0])
        ycomb[i, 0] = (part[i, rows(one, HB), :] + yrm[i, 0].astype(f32)).astype(bf16)
        send(ycomb.at[i, 0], yrm.at[i, 1], c_s, cm_r.at[i, 1], up)
        arrived(yrp.at[i, 0], cp_r.at[i, 0])
        ycomb[i, 1] = (part[i, rows(back + HB, HB), :] + yrp[i, 0].astype(f32)).astype(bf16)
        send(ycomb.at[i, 1], yrp.at[i, 1], c_s, cp_r.at[i, 1], down)

    def reduce_y_end(i):
        for h in (1, 2):
            arrived(yrm.at[i, h], cm_r.at[i, h])
            arrived(yrp.at[i, h], cp_r.at[i, h])
        ysum[i, 0] = part[i, rows(y * YB, HB), :] + yrm[i, 1].astype(f32) + yrp[i, 2].astype(f32)
        ysum[i, 1] = part[i, rows(y * YB + HB, HB), :] + yrm[i, 2].astype(f32) + yrp[i, 1].astype(f32)
        zsend[i] = ysum[i, 1 - zh].astype(bf16)
        send(zsend.at[i], zrecv.at[i], d_s, d_r.at[i], far)

    def activate(i):
        arrived(zrecv.at[i], d_r.at[i])
        a, p = i // PAIRS, i % PAIRS
        here = rows(y * YB + zh * HB, HB)

        @pl.loop(0, W // TILE)
        def _(n):
            value = ysum[i, zh, :, columns(n)] + zrecv[i, :, columns(n)].astype(f32)
            if a == 0:
                hid[p, :, columns(n)] = value
                inner = tanh_scale * (value + cube_weight * value * value * value)
                result = 0.5 * value * (1.0 + jnp.tanh(inner))
            else:
                h = hid[p, :, columns(n)]
                t = jnp.tanh(tanh_scale * (h + cube_weight * h * h * h))
                slope = 0.5 * (1.0 + t) + 0.5 * h * (1.0 - t * t) * tanh_scale * (
                    1.0 + 3.0 * cube_weight * h * h
                )
                result = value * slope
            ag[i, here, columns(n)] = result.astype(bf16)

        block = ag.at[i, here]
        send(block, block, f_s, f_r.at[i], far)
        send(block, block, g_s, gm_r.at[i, 0], up)
        send(block, block, g_s, gp_r.at[i, 0], down)

    def gather_y_middle(i):
        block = ag.at[i, rows(y * YB + (1 - zh) * HB, HB)]
        arrived(block, f_r.at[i])
        send(block, block, g_s, gm_r.at[i, 1], up)
        send(block, block, g_s, gp_r.at[i, 1], down)

    def gather_y_up(i):
        block = ag.at[i, rows(ring(y, 3) * YB + zh * HB, HB)]
        arrived(block, gm_r.at[i, 0])
        send(block, block, g_s, gm_r.at[i, 2], up)

    def gather_y_down(i):
        block = ag.at[i, rows(ring(y, 1) * YB + (1 - zh) * HB, HB)]
        arrived(block, gp_r.at[i, 1])
        send(block, block, g_s, gp_r.at[i, 2], down)

    def second_matmul(i):
        arrived(ag.at[i, rows(ring(y, 3) * YB + (1 - zh) * HB, HB)], gm_r.at[i, 1])
        arrived(ag.at[i, rows(ring(y, 1) * YB + zh * HB, HB)], gp_r.at[i, 0])
        arrived(ag.at[i, rows(ring(y, 2) * YB + zh * HB, HB)], gm_r.at[i, 2])
        arrived(ag.at[i, rows(ring(y, 2) * YB + (1 - zh) * HB, HB)], gp_r.at[i, 2])
        weight = (wo, wit)[i // PAIRS]
        loaded(1 - i // PAIRS)

        part[i] = jnp.dot(ag[i], weight[...], preferred_element_type=f32)

        send(
            part.at[i, rows((1 - core) * (M // 2), M // 2)], crecv.at[i],
            ic_s, ic_r.at[i], sibling,
        )

    def reduce_x_start(i):
        arrived(crecv.at[i], ic_r.at[i])

        @pl.loop(0, 4)
        def _(b):
            value = part[i, rows(core * (M // 2) + b * XB, XB), :] + crecv[i, rows(b * XB, XB), :]
            crecv[i, rows(b * XB, XB), :] = value
            xsend[i, rows(b * XB, XB), :] = value.astype(bf16)

        for k in (1, 2, 3):
            block = xsend.at[i, rows(ring(x, k) * XB, XB)]
            send(block, xrecv.at[i, x], ix_s, ix_r.at[i, x], xs[k - 1])

    def reduce_x_end(i):
        for k in (1, 2, 3):
            other = ring(x, k)
            arrived(xrecv.at[i, other], ix_r.at[i, other])
        total = crecv[i, rows(x * XB, XB), :]
        for k in (1, 2, 3):
            total = total + xrecv[i, ring(x, k)].astype(f32)
        a, k = i // PAIRS, i % PAIRS
        if k == 0:
            zrsum[a] = total
        else:
            zosend[a, k] = total.astype(bf16)
            send(zosend.at[a, k], zorecv.at[a, k], iz_s, iz_r.at[a, k], zs[k - 1])

    def reduce_z(a):
        total = zrsum[a]
        for k in (1, 2, 3):
            arrived(zorecv.at[a, k], iz_r.at[a, k])
            total = total + zorecv[a, k].astype(f32)
        out[a] = total.astype(bf16)

    def turn_out():
        loaded(1)

        @pl.loop(0, W // TILE)
        def _(n):
            wot[:, columns(n)] = wo[columns(n), :].T

    def turn_in():
        loaded(0)

        @pl.loop(0, W // TILE)
        def _(n):
            wit[:, columns(n)] = wi[columns(n), :].T

    def turn(k):
        (turn_out, turn_in)[k]()

    stages = (
        spread_z, spread_x, forward_x, spread_core, first_matmul,
        reduce_y_start, reduce_y_middle, reduce_y_end, activate,
        gather_y_middle, gather_y_up, gather_y_down,
        second_matmul, reduce_x_start, reduce_x_end, reduce_z, turn,
    )
    for code in ORDER:
        stages[code // 10](code % 10)
    for sem, ref in (
        (az_s, xg.at[0, pl.ds(0, 6 * R)]),
        (ax_s, xg.at[pl.ds(0, 3)]),
        (ac_s, xg.at[pl.ds(0, 4)]),
        (c_s, xg.at[pl.ds(0, 6)]),
        (d_s, xg.at[0]),
        (f_s, xg.at[0]),
        (g_s, xg.at[pl.ds(0, 6)]),
        (ic_s, crecv),
        (ix_s, xg.at[pl.ds(0, 3)]),
        (iz_s, xg.at[0, pl.ds(0, 6 * R)]),
    ):
        arrived(ref, sem)


def on_device(tokens, weight_in, weight_out, grad_out):
    vmem = pltpu.VMEM
    dma = pltpu.SemaphoreType.DMA
    block = jax.ShapeDtypeStruct((2, R, W), bf16)
    both = pl.pallas_call(
        kernel,
        out_shape=block,
        in_specs=[pl.BlockSpec(memory_space=pl.ANY)] * 4,
        out_specs=pl.BlockSpec(memory_space=vmem),
        scratch_shapes=[
            vmem((W, W), bf16),
            vmem((W, W), bf16),
            vmem((W, W), bf16),
            vmem((W, W), bf16),
            vmem((N, M, W), bf16),
            vmem((N, M, W), f32),
            vmem((N, M, W), bf16),
            vmem((N, 3, HB, W), bf16),
            vmem((N, 3, HB, W), bf16),
            vmem((N, 2, HB, W), bf16),
            vmem((N, 2, HB, W), f32),
            vmem((N, HB, W), bf16),
            vmem((N, HB, W), bf16),
            vmem((PAIRS, HB, W), f32),
            vmem((N, M, W), bf16),
            vmem((N, M // 2, W), f32),
            vmem((N, M // 2, W), bf16),
            vmem((N, 4, XB, W), bf16),
            vmem((2, R, W), f32),
            vmem((2, 4, R, W), bf16),
            vmem((2, 4, R, W), bf16),
            dma((2,)), dma((2,)),
            dma, dma((2, 4)),
            dma, dma((N, 3)),
            dma, dma((N,)),
            dma, dma((N, 3)), dma((N, 3)),
            dma, dma((N,)),
            dma, dma((N,)),
            dma, dma((N, 3)), dma((N, 3)),
            dma, dma((N,)),
            dma, dma((N, 4)),
            dma, dma((2, 4)),
        ],
        compiler_params=pltpu.CompilerParams(
            collective_id=0, has_side_effects=True, vmem_limit_bytes=60 * 1024 * 1024
        ),
        cost_estimate=pl.CostEstimate(
            flops=8 * 512 * W * W, bytes_accessed=4 * W * W, transcendentals=2 * 64 * W
        ),
        name="feed_forward",
    )(tokens, grad_out, weight_in, weight_out)
    return both[0].astype(bf16), both[1].astype(bf16)


def solution(mesh):
    placed = (P("row", "col"), P("col", "row"), P("row", "col"), P("row", "col"))
    return jax.shard_map(
        on_device,
        mesh=mesh,
        in_specs=placed,
        out_specs=(P("row", "col"), P("row", "col")),
        check_vma=False,
    )
```

```python
import functools

import jax
import jax.numpy as jnp
from jax import lax
from jax.experimental import pallas as pl
from jax.experimental.pallas import tpu as pltpu
from jax.sharding import PartitionSpec as P

MESH = pl.DeviceIdType.MESH
f32, bf16 = jnp.float32, jnp.bfloat16
tanh_scale = 0.7978845608028654
cube_weight = 0.044715

W = 1536
R = 16
PAIRS = 4
N = 2 * PAIRS
M = 128
XB, YB, HB = M // 8, M // 4, M // 8
TILE = 512
ORDER = (
    1, 10, 2, 3, 7, 14, 20, 6, 12, 150, 24, 30, 40, 13, 34, 5, 44, 22,
    17, 11, 50, 32, 42, 23, 16, 15, 54, 27, 33, 43, 60, 52, 21, 37, 47, 64,
    31, 53, 26, 62, 41, 25, 57, 70, 36, 63, 46, 35, 67, 72, 51, 56, 151, 45,
    73, 80, 61, 66, 55, 77, 82, 90, 83, 65, 100, 71, 76, 103, 93, 92, 87, 97,
    110, 102, 75, 74, 91, 96, 81, 120, 113, 107, 86, 112, 101, 123, 85, 117, 106, 122,
    84, 95, 111, 105, 127, 94, 130, 133, 116, 104, 132, 121, 115, 137, 126, 114, 131, 125,
    136, 124, 140, 135, 134, 141,
)


def columns(step):
    return pl.ds(pl.multiple_of(step * TILE, TILE), TILE)


def rows(start, size):
    return pl.ds(pl.multiple_of(start, R), size)


def kernel(
    tok, grad, wi_hbm, wo_hbm, out,
    wi, wo, wit, wot, xg, part, ysend, yrm, yrp, ycomb, ysum, zsend, zrecv, hid, ag,
    crecv, xsend, xrecv, zrsum, zosend, zorecv,
    w_sem, own_sem, az_s, az_r, ax_s, ax_r, ac_s, ac_r, c_s, cm_r, cp_r, d_s, d_r, f_s, f_r,
    g_s, gm_r, gp_r, ic_s, ic_r, ix_s, ix_r, iz_s, iz_r,
):
    row, col = lax.axis_index("row"), lax.axis_index("col")
    core, x, zl = row % 2, (row // 2) % 4, row // 8
    y, zh = col // 2, col % 2

    def device(x=x, zl=zl, core=core, y=y, zh=zh):
        return ((zl * 4 + x) * 2 + core, y * 2 + zh)

    def ring(i, k):
        return (i + k) % 4

    xs = [device(x=ring(x, k)) for k in (1, 2, 3)]
    zs = [
        device(zl=plane)
        for plane in (zl + 1 - 2 * (zl % 2), zl + 2 - 4 * (zl // 2), 3 - zl)
    ]
    sibling = device(core=1 - core)
    up, down = device(y=ring(y, 1)), device(y=ring(y, 3))
    far = device(zh=1 - zh)

    def send(src, dst, s_sem, r_sem, to):
        copy = pltpu.make_async_remote_copy(
            src_ref=src, dst_ref=dst, send_sem=s_sem, recv_sem=r_sem,
            device_id=to, device_id_type=MESH,
        )
        copy.start()

    def arrived(ref, sem):
        pltpu.make_async_copy(ref, ref, sem).wait()

    waited = set()

    def loaded(k):
        if k not in waited:
            waited.add(k)
            loads[k].wait()

    mine = rows(core * (M // 2) + x * XB, XB)
    barrier = pltpu.get_barrier_semaphore()
    for to in [far] + zs + xs + [up, down, sibling]:
        pl.semaphore_signal(barrier, inc=1, device_id=to, device_id_type=MESH)
    own = [
        pltpu.make_async_copy(src, xg.at[a * PAIRS, mine], own_sem.at[a])
        for a, src in enumerate((tok, grad))
    ]
    for copy in own:
        copy.start()
    loads = [
        pltpu.make_async_copy(wi_hbm, wi, w_sem.at[0]),
        pltpu.make_async_copy(wo_hbm, wo, w_sem.at[1]),
    ]
    for load in loads:
        load.start()
    for copy in own:
        copy.wait()
    pl.semaphore_wait(barrier, 10)

    def spread_z(i):
        a, k = i // PAIRS, i % PAIRS
        send(xg.at[a * PAIRS, mine], xg.at[i, mine], az_s, az_r.at[a, k], zs[k - 1])

    def spread_x(i):
        a, k = i // PAIRS, i % PAIRS
        block = xg.at[i, mine]
        if k > 0:
            arrived(block, az_r.at[a, k])
        send(block, block, ax_s, ax_r.at[i, 0], xs[0])
        send(block, block, ax_s, ax_r.at[i, 1], xs[2])
        send(block, block, ax_s, ax_r.at[i, 2], xs[1])

    def spread_core(i):
        for k in (0, 1):
            arrived(xg.at[i, rows(core * (M // 2) + ring(x, 3 - 2 * k) * XB, XB)], ax_r.at[i, k])
        arrived(xg.at[i, rows(core * (M // 2) + ring(x, 2) * XB, XB)], ax_r.at[i, 2])
        half = xg.at[i, rows(core * (M // 2), M // 2)]
        send(half, half, ac_s, ac_r.at[i], sibling)

    def first_matmul(i):
        arrived(xg.at[i, rows((1 - core) * (M // 2), M // 2)], ac_r.at[i])
        weight = (wi, wot)[i // PAIRS]
        loaded(i // PAIRS)

        value = jnp.dot(xg[i], weight[...], preferred_element_type=f32)
        part[i] = value
        ysend[i] = value.astype(bf16)

    def reduce_y_start(i):
        two, one, back = ring(y, 2) * YB, ring(y, 1) * YB, ring(y, 3) * YB
        send(ysend.at[i, rows(two, HB)], yrm.at[i, 0], c_s, cm_r.at[i, 0], up)
        send(ysend.at[i, rows(two + HB, HB)], yrp.at[i, 0], c_s, cp_r.at[i, 0], down)
        send(ysend.at[i, rows(one + HB, HB)], yrm.at[i, 2], c_s, cm_r.at[i, 2], up)
        send(ysend.at[i, rows(back, HB)], yrp.at[i, 2], c_s, cp_r.at[i, 2], down)

    def reduce_y_middle(i):
        one, back = ring(y, 1) * YB, ring(y, 3) * YB
        arrived(yrm.at[i, 0], cm_r.at[i, 0])
        ycomb[i, 0] = (part[i, rows(one, HB), :] + yrm[i, 0].astype(f32)).astype(bf16)
        send(ycomb.at[i, 0], yrm.at[i, 1], c_s, cm_r.at[i, 1], up)
        arrived(yrp.at[i, 0], cp_r.at[i, 0])
        ycomb[i, 1] = (part[i, rows(back + HB, HB), :] + yrp[i, 0].astype(f32)).astype(bf16)
        send(ycomb.at[i, 1], yrp.at[i, 1], c_s, cp_r.at[i, 1], down)

    def reduce_y_end(i):
        for h in (1, 2):
            arrived(yrm.at[i, h], cm_r.at[i, h])
            arrived(yrp.at[i, h], cp_r.at[i, h])
        ysum[i, 0] = part[i, rows(y * YB, HB), :] + yrm[i, 1].astype(f32) + yrp[i, 2].astype(f32)
        ysum[i, 1] = part[i, rows(y * YB + HB, HB), :] + yrm[i, 2].astype(f32) + yrp[i, 1].astype(f32)
        zsend[i] = ysum[i, 1 - zh].astype(bf16)
        send(zsend.at[i], zrecv.at[i], d_s, d_r.at[i], far)

    def activate(i):
        arrived(zrecv.at[i], d_r.at[i])
        a, p = i // PAIRS, i % PAIRS
        here = rows(y * YB + zh * HB, HB)

        @pl.loop(0, W // TILE)
        def _(n):
            value = ysum[i, zh, :, columns(n)] + zrecv[i, :, columns(n)].astype(f32)
            if a == 0:
                hid[p, :, columns(n)] = value
                inner = tanh_scale * (value + cube_weight * value * value * value)
                result = 0.5 * value * (1.0 + jnp.tanh(inner))
            else:
                h = hid[p, :, columns(n)]
                t = jnp.tanh(tanh_scale * (h + cube_weight * h * h * h))
                slope = 0.5 * (1.0 + t) + 0.5 * h * (1.0 - t * t) * tanh_scale * (
                    1.0 + 3.0 * cube_weight * h * h
                )
                result = value * slope
            ag[i, here, columns(n)] = result.astype(bf16)

        block = ag.at[i, here]
        send(block, block, f_s, f_r.at[i], far)
        send(block, block, g_s, gm_r.at[i, 0], up)
        send(block, block, g_s, gp_r.at[i, 0], down)

    def gather_y_middle(i):
        block = ag.at[i, rows(y * YB + (1 - zh) * HB, HB)]
        arrived(block, f_r.at[i])
        send(block, block, g_s, gm_r.at[i, 1], up)
        send(block, block, g_s, gp_r.at[i, 1], down)

    def gather_y_up(i):
        block = ag.at[i, rows(ring(y, 3) * YB + zh * HB, HB)]
        arrived(block, gm_r.at[i, 0])
        send(block, block, g_s, gm_r.at[i, 2], up)

    def gather_y_down(i):
        block = ag.at[i, rows(ring(y, 1) * YB + (1 - zh) * HB, HB)]
        arrived(block, gp_r.at[i, 1])
        send(block, block, g_s, gp_r.at[i, 2], down)

    def second_matmul(i):
        arrived(ag.at[i, rows(ring(y, 3) * YB + (1 - zh) * HB, HB)], gm_r.at[i, 1])
        arrived(ag.at[i, rows(ring(y, 1) * YB + zh * HB, HB)], gp_r.at[i, 0])
        arrived(ag.at[i, rows(ring(y, 2) * YB + zh * HB, HB)], gm_r.at[i, 2])
        arrived(ag.at[i, rows(ring(y, 2) * YB + (1 - zh) * HB, HB)], gp_r.at[i, 2])
        weight = (wo, wit)[i // PAIRS]
        loaded(1 - i // PAIRS)

        part[i] = jnp.dot(ag[i], weight[...], preferred_element_type=f32)

        send(
            part.at[i, rows((1 - core) * (M // 2), M // 2)], crecv.at[i],
            ic_s, ic_r.at[i], sibling,
        )

    def reduce_x_start(i):
        arrived(crecv.at[i], ic_r.at[i])

        @pl.loop(0, 4)
        def _(b):
            value = part[i, rows(core * (M // 2) + b * XB, XB), :] + crecv[i, rows(b * XB, XB), :]
            crecv[i, rows(b * XB, XB), :] = value
            xsend[i, rows(b * XB, XB), :] = value.astype(bf16)

        for k in (1, 2, 3):
            block = xsend.at[i, rows(ring(x, k) * XB, XB)]
            send(block, xrecv.at[i, x], ix_s, ix_r.at[i, x], xs[k - 1])

    def reduce_x_end(i):
        for k in (1, 2, 3):
            other = ring(x, k)
            arrived(xrecv.at[i, other], ix_r.at[i, other])
        total = crecv[i, rows(x * XB, XB), :]
        for k in (1, 2, 3):
            total = total + xrecv[i, ring(x, k)].astype(f32)
        a, k = i // PAIRS, i % PAIRS
        if k == 0:
            zrsum[a] = total
        else:
            zosend[a, k] = total.astype(bf16)
            send(zosend.at[a, k], zorecv.at[a, k], iz_s, iz_r.at[a, k], zs[k - 1])

    def reduce_z(a):
        total = zrsum[a]
        for k in (1, 2, 3):
            arrived(zorecv.at[a, k], iz_r.at[a, k])
            total = total + zorecv[a, k].astype(f32)
        out[a] = total.astype(bf16)

    def turn_out():
        loaded(1)

        @pl.loop(0, W // TILE)
        def _(n):
            wot[:, columns(n)] = wo[columns(n), :].T

    def turn_in():
        loaded(0)

        @pl.loop(0, W // TILE)
        def _(n):
            wit[:, columns(n)] = wi[columns(n), :].T

    def turn(k):
        (turn_out, turn_in)[k]()

    stages = (
        spread_z, spread_x, spread_core, first_matmul,
        reduce_y_start, reduce_y_middle, reduce_y_end, activate,
        gather_y_middle, gather_y_up, gather_y_down,
        second_matmul, reduce_x_start, reduce_x_end, reduce_z, turn,
    )

    def wait_sends():
        for sem, ref in (
            (az_s, xg.at[0, pl.ds(0, 6 * R)]),
            (ax_s, xg.at[pl.ds(0, 3)]),
            (ac_s, xg.at[pl.ds(0, 4)]),
            (c_s, xg.at[pl.ds(0, 6)]),
            (d_s, xg.at[0]),
            (f_s, xg.at[0]),
            (g_s, xg.at[pl.ds(0, 6)]),
            (ic_s, crecv),
            (ix_s, xg.at[pl.ds(0, 3)]),
            (iz_s, xg.at[0, pl.ds(0, 6 * R)]),
        ):
            arrived(ref, sem)

    for code in ORDER:
        if code == ORDER[-1]:
            wait_sends()
        stages[code // 10](code % 10)


def on_device(tokens, weight_in, weight_out, grad_out):
    vmem = pltpu.VMEM
    dma = pltpu.SemaphoreType.DMA
    block = jax.ShapeDtypeStruct((2, R, W), bf16)
    both = pl.pallas_call(
        kernel,
        out_shape=block,
        in_specs=[pl.BlockSpec(memory_space=pl.ANY)] * 4,
        out_specs=pl.BlockSpec(memory_space=vmem),
        scratch_shapes=[
            vmem((W, W), bf16),
            vmem((W, W), bf16),
            vmem((W, W), bf16),
            vmem((W, W), bf16),
            vmem((N, M, W), bf16),
            vmem((N, M, W), f32),
            vmem((N, M, W), bf16),
            vmem((N, 3, HB, W), bf16),
            vmem((N, 3, HB, W), bf16),
            vmem((N, 2, HB, W), bf16),
            vmem((N, 2, HB, W), f32),
            vmem((N, HB, W), bf16),
            vmem((N, HB, W), bf16),
            vmem((PAIRS, HB, W), f32),
            vmem((N, M, W), bf16),
            vmem((N, M // 2, W), f32),
            vmem((N, M // 2, W), bf16),
            vmem((N, 4, XB, W), bf16),
            vmem((2, R, W), f32),
            vmem((2, 4, R, W), bf16),
            vmem((2, 4, R, W), bf16),
            dma((2,)), dma((2,)),
            dma, dma((2, 4)),
            dma, dma((N, 3)),
            dma, dma((N,)),
            dma, dma((N, 3)), dma((N, 3)),
            dma, dma((N,)),
            dma, dma((N,)),
            dma, dma((N, 3)), dma((N, 3)),
            dma, dma((N,)),
            dma, dma((N, 4)),
            dma, dma((2, 4)),
        ],
        compiler_params=pltpu.CompilerParams(
            collective_id=0, has_side_effects=True, vmem_limit_bytes=60 * 1024 * 1024
        ),
        cost_estimate=pl.CostEstimate(
            flops=8 * 512 * W * W, bytes_accessed=4 * W * W, transcendentals=2 * 64 * W
        ),
        name="feed_forward",
    )(tokens, grad_out, weight_in, weight_out)
    return both[0].astype(bf16), both[1].astype(bf16)


def solution(mesh):
    placed = (P("row", "col"), P("col", "row"), P("row", "col"), P("row", "col"))
    return jax.shard_map(
        on_device,
        mesh=mesh,
        in_specs=placed,
        out_specs=(P("row", "col"), P("row", "col")),
        check_vma=False,
    )
```

```python
import functools

import jax
import jax.numpy as jnp
from jax import lax
from jax.experimental import pallas as pl
from jax.experimental.pallas import tpu as pltpu
from jax.sharding import PartitionSpec as P

MESH = pl.DeviceIdType.MESH
f32, bf16 = jnp.float32, jnp.bfloat16
tanh_scale = 0.7978845608028654
cube_weight = 0.044715

W = 1536
R = 16
PAIRS = 4
N = 2 * PAIRS
M = 128
XB, YB, HB = M // 8, M // 4, M // 8
TILE = 512
ORDER = (
    1, 10, 2, 3, 14, 5, 20, 7, 12, 150, 24, 30, 40, 13, 6, 11, 15, 34,
    44, 22, 17, 50, 32, 42, 23, 54, 16, 60, 21, 52, 33, 43, 31, 41, 25, 64,
    27, 53, 62, 37, 47, 26, 70, 51, 63, 36, 46, 72, 35, 61, 57, 45, 73, 67,
    56, 80, 55, 82, 92, 90, 71, 66, 100, 65, 83, 77, 102, 81, 110, 93, 76, 151,
    103, 97, 75, 91, 74, 112, 120, 87, 101, 86, 113, 122, 95, 107, 96, 85, 111, 106,
    84, 123, 117, 105, 132, 94, 121, 116, 104, 127, 133, 115, 126, 130, 114, 137, 125, 136,
    124, 131, 135, 134, 140, 141,
)


def columns(step):
    return pl.ds(pl.multiple_of(step * TILE, TILE), TILE)


def rows(start, size):
    return pl.ds(pl.multiple_of(start, R), size)


def kernel(
    tok, grad, wi_hbm, wo_hbm, out,
    wi, wo, wit, wot, xg, part, ysend, yrm, yrp, ycomb, ysum, zsend, zrecv, hid, ag,
    crecv, xsend, xrecv, zrsum, zosend, zorecv,
    w_sem, own_sem, az_s, az_r, ax_s, ax_r, ac_s, ac_r, c_s, cm_r, cp_r, d_s, d_r, f_s, f_r,
    g_s, gm_r, gp_r, ic_s, ic_r, ix_s, ix_r, iz_s, iz_r,
):
    row, col = lax.axis_index("row"), lax.axis_index("col")
    core, x, zl = row % 2, (row // 2) % 4, row // 8
    y, zh = col // 2, col % 2

    def device(x=x, zl=zl, core=core, y=y, zh=zh):
        return ((zl * 4 + x) * 2 + core, y * 2 + zh)

    def ring(i, k):
        return (i + k) % 4

    xs = [device(x=ring(x, k)) for k in (1, 2, 3)]
    zs = [
        device(zl=plane)
        for plane in (zl + 1 - 2 * (zl % 2), zl + 2 - 4 * (zl // 2), 3 - zl)
    ]
    sibling = device(core=1 - core)
    up, down = device(y=ring(y, 1)), device(y=ring(y, 3))
    far = device(zh=1 - zh)

    def send(src, dst, s_sem, r_sem, to):
        copy = pltpu.make_async_remote_copy(
            src_ref=src, dst_ref=dst, send_sem=s_sem, recv_sem=r_sem,
            device_id=to, device_id_type=MESH,
        )
        copy.start()

    def arrived(ref, sem):
        pltpu.make_async_copy(ref, ref, sem).wait()

    waited = set()

    def loaded(k):
        if k not in waited:
            waited.add(k)
            loads[k].wait()

    mine = rows(core * (M // 2) + x * XB, XB)
    barrier = pltpu.get_barrier_semaphore()
    for to in [far] + zs + xs + [up, down, sibling]:
        pl.semaphore_signal(barrier, inc=1, device_id=to, device_id_type=MESH)
    own = [
        pltpu.make_async_copy(src, xg.at[a * PAIRS, mine], own_sem.at[a])
        for a, src in enumerate((tok, grad))
    ]
    for copy in own:
        copy.start()
    loads = [
        pltpu.make_async_copy(wi_hbm, wi, w_sem.at[0]),
        pltpu.make_async_copy(wo_hbm, wo, w_sem.at[1]),
    ]
    for load in loads:
        load.start()
    for copy in own:
        copy.wait()
    pl.semaphore_wait(barrier, 10)

    def spread_z(i):
        a, k = i // PAIRS, i % PAIRS
        send(xg.at[a * PAIRS, mine], xg.at[i, mine], az_s, az_r.at[a, k], zs[k - 1])

    def spread_x(i):
        a, k = i // PAIRS, i % PAIRS
        block = xg.at[i, mine]
        if k > 0:
            arrived(block, az_r.at[a, k])
        send(block, block, ax_s, ax_r.at[i, 0], xs[0])
        send(block, block, ax_s, ax_r.at[i, 1], xs[2])
        send(block, block, ax_s, ax_r.at[i, 2], xs[1])

    def spread_core(i):
        for k in (0, 1):
            arrived(xg.at[i, rows(core * (M // 2) + ring(x, 3 - 2 * k) * XB, XB)], ax_r.at[i, k])
        arrived(xg.at[i, rows(core * (M // 2) + ring(x, 2) * XB, XB)], ax_r.at[i, 2])
        half = xg.at[i, rows(core * (M // 2), M // 2)]
        send(half, half, ac_s, ac_r.at[i], sibling)

    def first_matmul(i):
        arrived(xg.at[i, rows((1 - core) * (M // 2), M // 2)], ac_r.at[i])
        weight = (wi, wot)[i // PAIRS]
        loaded(i // PAIRS)

        value = jnp.dot(xg[i], weight[...], preferred_element_type=f32)
        part[i] = value
        ysend[i] = value.astype(bf16)

    def reduce_y_start(i):
        two, one, back = ring(y, 2) * YB, ring(y, 1) * YB, ring(y, 3) * YB
        send(ysend.at[i, rows(two, HB)], yrm.at[i, 0], c_s, cm_r.at[i, 0], up)
        send(ysend.at[i, rows(two + HB, HB)], yrp.at[i, 0], c_s, cp_r.at[i, 0], down)
        send(ysend.at[i, rows(one + HB, HB)], yrm.at[i, 2], c_s, cm_r.at[i, 2], up)
        send(ysend.at[i, rows(back, HB)], yrp.at[i, 2], c_s, cp_r.at[i, 2], down)

    def reduce_y_middle(i):
        one, back = ring(y, 1) * YB, ring(y, 3) * YB
        arrived(yrm.at[i, 0], cm_r.at[i, 0])
        ycomb[i, 0] = (part[i, rows(one, HB), :] + yrm[i, 0].astype(f32)).astype(bf16)
        send(ycomb.at[i, 0], yrm.at[i, 1], c_s, cm_r.at[i, 1], up)
        arrived(yrp.at[i, 0], cp_r.at[i, 0])
        ycomb[i, 1] = (part[i, rows(back + HB, HB), :] + yrp[i, 0].astype(f32)).astype(bf16)
        send(ycomb.at[i, 1], yrp.at[i, 1], c_s, cp_r.at[i, 1], down)

    def reduce_y_end(i):
        for h in (1, 2):
            arrived(yrm.at[i, h], cm_r.at[i, h])
            arrived(yrp.at[i, h], cp_r.at[i, h])
        ysum[i, 0] = part[i, rows(y * YB, HB), :] + yrm[i, 1].astype(f32) + yrp[i, 2].astype(f32)
        ysum[i, 1] = part[i, rows(y * YB + HB, HB), :] + yrm[i, 2].astype(f32) + yrp[i, 1].astype(f32)
        zsend[i] = ysum[i, 1 - zh].astype(bf16)
        send(zsend.at[i], zrecv.at[i], d_s, d_r.at[i], far)

    def activate(i):
        arrived(zrecv.at[i], d_r.at[i])
        a, p = i // PAIRS, i % PAIRS
        here = rows(y * YB + zh * HB, HB)

        @pl.loop(0, W // TILE)
        def _(n):
            value = ysum[i, zh, :, columns(n)] + zrecv[i, :, columns(n)].astype(f32)
            if a == 0:
                hid[p, :, columns(n)] = value
                inner = tanh_scale * (value + cube_weight * value * value * value)
                result = 0.5 * value * (1.0 + jnp.tanh(inner))
            else:
                h = hid[p, :, columns(n)]
                t = jnp.tanh(tanh_scale * (h + cube_weight * h * h * h))
                slope = 0.5 * (1.0 + t) + 0.5 * h * (1.0 - t * t) * tanh_scale * (
                    1.0 + 3.0 * cube_weight * h * h
                )
                result = value * slope
            ag[i, here, columns(n)] = result.astype(bf16)

        block = ag.at[i, here]
        send(block, block, f_s, f_r.at[i], far)
        send(block, block, g_s, gm_r.at[i, 0], up)
        send(block, block, g_s, gp_r.at[i, 0], down)

    def gather_y_middle(i):
        block = ag.at[i, rows(y * YB + (1 - zh) * HB, HB)]
        arrived(block, f_r.at[i])
        send(block, block, g_s, gm_r.at[i, 1], up)
        send(block, block, g_s, gp_r.at[i, 1], down)

    def gather_y_up(i):
        block = ag.at[i, rows(ring(y, 3) * YB + zh * HB, HB)]
        arrived(block, gm_r.at[i, 0])
        send(block, block, g_s, gm_r.at[i, 2], up)

    def gather_y_down(i):
        block = ag.at[i, rows(ring(y, 1) * YB + (1 - zh) * HB, HB)]
        arrived(block, gp_r.at[i, 1])
        send(block, block, g_s, gp_r.at[i, 2], down)

    def second_matmul(i):
        arrived(ag.at[i, rows(ring(y, 3) * YB + (1 - zh) * HB, HB)], gm_r.at[i, 1])
        arrived(ag.at[i, rows(ring(y, 1) * YB + zh * HB, HB)], gp_r.at[i, 0])
        arrived(ag.at[i, rows(ring(y, 2) * YB + zh * HB, HB)], gm_r.at[i, 2])
        arrived(ag.at[i, rows(ring(y, 2) * YB + (1 - zh) * HB, HB)], gp_r.at[i, 2])
        weight = (wo, wit)[i // PAIRS]
        loaded(1 - i // PAIRS)

        part[i] = jnp.dot(ag[i], weight[...], preferred_element_type=f32)

        send(
            part.at[i, rows((1 - core) * (M // 2), M // 2)], crecv.at[i],
            ic_s, ic_r.at[i], sibling,
        )

    def reduce_x_start(i):
        arrived(crecv.at[i], ic_r.at[i])

        @pl.loop(0, 4)
        def _(b):
            value = part[i, rows(core * (M // 2) + b * XB, XB), :] + crecv[i, rows(b * XB, XB), :]
            crecv[i, rows(b * XB, XB), :] = value
            xsend[i, rows(b * XB, XB), :] = value.astype(bf16)

        for k in (1, 2, 3):
            block = xsend.at[i, rows(ring(x, k) * XB, XB)]
            send(block, xrecv.at[i, x], ix_s, ix_r.at[i, x], xs[k - 1])

    def reduce_x_end(i):
        for k in (1, 2, 3):
            other = ring(x, k)
            arrived(xrecv.at[i, other], ix_r.at[i, other])
        total = crecv[i, rows(x * XB, XB), :]
        for k in (1, 2, 3):
            total = total + xrecv[i, ring(x, k)].astype(f32)
        a, k = i // PAIRS, i % PAIRS
        if k == 0:
            zrsum[a] = total
        else:
            zosend[a, k] = total.astype(bf16)
            send(zosend.at[a, k], zorecv.at[a, k], iz_s, iz_r.at[a, k], zs[k - 1])

    def reduce_z(a):
        total = zrsum[a]
        for k in (1, 2, 3):
            arrived(zorecv.at[a, k], iz_r.at[a, k])
            total = total + zorecv[a, k].astype(f32)
        out[a] = total.astype(bf16)

    def turn_out():
        loaded(1)

        @pl.loop(0, W // TILE)
        def _(n):
            wot[:, columns(n)] = wo[columns(n), :].T

    def turn_in():
        loaded(0)

        @pl.loop(0, W // TILE)
        def _(n):
            wit[:, columns(n)] = wi[columns(n), :].T

    def turn(k):
        (turn_out, turn_in)[k]()

    stages = (
        spread_z, spread_x, spread_core, first_matmul,
        reduce_y_start, reduce_y_middle, reduce_y_end, activate,
        gather_y_middle, gather_y_up, gather_y_down,
        second_matmul, reduce_x_start, reduce_x_end, reduce_z, turn,
    )

    def wait_sends():
        for sem, ref in (
            (az_s, xg.at[0, pl.ds(0, 6 * R)]),
            (ax_s, xg.at[pl.ds(0, 3)]),
            (ac_s, xg.at[pl.ds(0, 4)]),
            (c_s, xg.at[pl.ds(0, 6)]),
            (d_s, xg.at[0]),
            (f_s, xg.at[0]),
            (g_s, xg.at[pl.ds(0, 6)]),
            (ic_s, crecv),
            (ix_s, xg.at[pl.ds(0, 3)]),
            (iz_s, xg.at[0, pl.ds(0, 6 * R)]),
        ):
            arrived(ref, sem)

    for code in ORDER:
        if code == ORDER[-1]:
            wait_sends()
        stages[code // 10](code % 10)


def on_device(tokens, weight_in, weight_out, grad_out):
    vmem = pltpu.VMEM
    dma = pltpu.SemaphoreType.DMA
    block = jax.ShapeDtypeStruct((2, R, W), bf16)
    both = pl.pallas_call(
        kernel,
        out_shape=block,
        in_specs=[pl.BlockSpec(memory_space=pl.ANY)] * 4,
        out_specs=pl.BlockSpec(memory_space=vmem),
        scratch_shapes=[
            vmem((W, W), bf16),
            vmem((W, W), bf16),
            vmem((W, W), bf16),
            vmem((W, W), bf16),
            vmem((N, M, W), bf16),
            vmem((N, M, W), f32),
            vmem((N, M, W), bf16),
            vmem((N, 3, HB, W), bf16),
            vmem((N, 3, HB, W), bf16),
            vmem((N, 2, HB, W), bf16),
            vmem((N, 2, HB, W), f32),
            vmem((N, HB, W), bf16),
            vmem((N, HB, W), bf16),
            vmem((PAIRS, HB, W), f32),
            vmem((N, M, W), bf16),
            vmem((N, M // 2, W), f32),
            vmem((N, M // 2, W), bf16),
            vmem((N, 4, XB, W), bf16),
            vmem((2, R, W), f32),
            vmem((2, 4, R, W), bf16),
            vmem((2, 4, R, W), bf16),
            dma((2,)), dma((2,)),
            dma, dma((2, 4)),
            dma, dma((N, 3)),
            dma, dma((N,)),
            dma, dma((N, 3)), dma((N, 3)),
            dma, dma((N,)),
            dma, dma((N,)),
            dma, dma((N, 3)), dma((N, 3)),
            dma, dma((N,)),
            dma, dma((N, 4)),
            dma, dma((2, 4)),
        ],
        compiler_params=pltpu.CompilerParams(
            collective_id=0, has_side_effects=True, vmem_limit_bytes=60 * 1024 * 1024
        ),
        cost_estimate=pl.CostEstimate(
            flops=8 * 512 * W * W, bytes_accessed=4 * W * W, transcendentals=2 * 64 * W
        ),
        name="feed_forward",
    )(tokens, grad_out, weight_in, weight_out)
    return both[0].astype(bf16), both[1].astype(bf16)


def solution(mesh):
    placed = (P("row", "col"), P("col", "row"), P("row", "col"), P("row", "col"))
    return jax.shard_map(
        on_device,
        mesh=mesh,
        in_specs=placed,
        out_specs=(P("row", "col"), P("row", "col")),
        check_vma=False,
    )
```
